32 devices in a mesh: groups: 2 (over y), rows: 8 (over z, x), blocks: 2 (over core).
Axes of the slice: x: 2, y: 2, z: 4, core: 2. Of those that a mesh axis runs over, the one named last changes fastest.
Arguments:
- adjoint_in: bfloat16 [16, 16, 256], P(('groups', 'rows')), parts along dimension 0, may hold values from -6 to 6
- far_u: bfloat16 [16, 2, 128, 32, 256], P(('groups', 'rows'), 'blocks'), parts along dimension 0, may hold values from -0.375 to 0.375
- far_v: bfloat16 [16, 2, 128, 32, 256], P(('groups', 'rows'), 'blocks'), parts along dimension 0, may hold values from -0.09375 to 0.09375
- far_cols: int32 [16, 2, 128], P(('groups', 'rows'), 'blocks'), parts along dimension 0, may hold values from 0 to 7, as said below
- far_counts: int32 [16, 2], P(('groups', 'rows'), 'blocks'), parts along dimension 0, may hold values from 96 to 128, as said below
- near_blocks: bfloat16 [16, 2, 4, 256, 256], P(('groups', 'rows'), 'blocks'), parts along dimension 0, may hold values from -0.125 to 0.125
- near_cols: int32 [16, 2, 4], P(('groups', 'rows'), 'blocks'), parts along dimension 0, may hold values from 0 to 7, as said below
Outputs:
- adjoint_out: float32 [16, 16, 256], P(('groups', 'rows'), 'blocks'), parts along dimension 0
The draws below stay inside these ranges and needn't reach their ends.
There are 2 independent parts, one for each index of `groups`. The reference program is written for one: setup_inputs(seed, part) draws one part's arguments, and reference() takes and returns one part's arrays. A program takes and returns all parts, laid end to end along the dimension named above; each array names one. Nothing has to cross between parts.
Inputs may be any that keep to these rules, and one draw needn't show every extreme that they name: `far_cols`: among the first far_counts[r, b] slots of one (r, b), no column cluster is named more than 16 times; in every draw one column cluster is named by the first 16 slots of every (r, b). `far_counts`: some (r, b) has exactly 128 live slots. near_cols[r, b, j] differs from r by at most one.
All inputs are finite; a program needn't handle non-finite values.
Results may differ from the reference program's by a relative error of at most 0.0023.
Values may be sent and summed in bfloat16 or wider, within the bound.
A program may use at most 64 MiB of HBM per device.

```python
import jax
import jax.numpy as jnp
from jax import lax

LEAF = 256
RANK = 32
R = 16
FAR_HALF = 128
NEAR_HALF = 4
NCL = 8
CAP = 16
N_BLOCKS = 2


def draw_far_cols(key, part):
    key = jax.random.fold_in(key, 11)
    star_key, device_key = jax.random.split(key)
    crowded = jax.random.randint(star_key, (), 0, NCL).astype(jnp.int32)
    repeats = (FAR_HALF - CAP + NCL - 2) // (NCL - 1)
    device_keys = jax.random.split(device_key, NCL * N_BLOCKS)

    def one_device(sub_key):
        others = jax.random.permutation(sub_key, NCL - 1).astype(jnp.int32)
        tiled = jnp.tile(others, repeats)[:FAR_HALF - CAP]
        tiled = tiled + (tiled >= crowded).astype(jnp.int32)
        return jnp.concatenate([jnp.full((CAP,), crowded, dtype=jnp.int32), tiled])
    return jax.vmap(one_device)(device_keys).reshape(NCL, N_BLOCKS, FAR_HALF)


def draw_far_counts(key, part):
    key = jax.random.fold_in(key, 23)
    count_key, full_key = jax.random.split(key)
    lowest = FAR_HALF - FAR_HALF // 4
    drawn = jax.random.randint(count_key, (NCL * N_BLOCKS,), lowest, FAR_HALF + 1).astype(jnp.int32)
    fullest = jax.random.randint(full_key, (), 0, NCL * N_BLOCKS)
    drawn = jnp.where(jnp.arange(NCL * N_BLOCKS) == fullest, FAR_HALF, drawn)
    return drawn.reshape(NCL, N_BLOCKS).astype(jnp.int32)


def draw_near_cols(key, part):
    key = jax.random.fold_in(key, 37)
    offsets = jax.random.randint(key, (NCL, N_BLOCKS, NEAR_HALF), -1, 2).astype(jnp.int32)
    row_index = jnp.arange(NCL, dtype=jnp.int32)[:, None, None]
    return jnp.clip(row_index + offsets, 0, NCL - 1).astype(jnp.int32)


def levels(rng, dims, shards, smallest, top_value):
    gain = 1.0
    for dim, blocks in shards:
        heights = jax.random.uniform(jax.random.fold_in(jax.random.fold_in(rng, 6), dim), (blocks,), jnp.float32, smallest / len(shards), top_value / len(shards))
        gain = gain * jnp.repeat(jnp.exp(heights), dims[dim] // blocks).reshape((-1,) + (1,) * (len(dims) - 1 - dim))
    return gain


def scatter_about(rng, dims, width, reach, cuts=(), kind=jnp.bfloat16):
    values = width * jax.random.normal(rng, dims, jnp.float32)
    if cuts:
        values = values * levels(rng, dims, cuts, -0.22, 0.18)
    return jnp.clip(values, -reach, reach).astype(kind)


def setup_inputs(seed: int = 0, part: int = 0) -> dict:
    keys = jax.random.split(jax.random.key(seed), 8)
    own_keys = jax.random.split(jax.random.fold_in(keys[7], part), 8)
    adjoint_in = scatter_about(own_keys[0], (NCL, R, LEAF), 1.0, 6.0, ((0, 8),))
    far_u = scatter_about(own_keys[1], (NCL, N_BLOCKS, FAR_HALF, RANK, LEAF), LEAF ** -0.5, 0.375, ((0, 8), (1, 2)))
    far_v = scatter_about(own_keys[2], (NCL, N_BLOCKS, FAR_HALF, RANK, LEAF), (RANK * FAR_HALF) ** -0.5, 0.09375, ((0, 8), (1, 2)))
    far_cols = draw_far_cols(jax.random.fold_in(jax.random.fold_in(keys[7], part), 71), part)
    far_counts = draw_far_counts(jax.random.fold_in(jax.random.fold_in(keys[7], part), 71), part)
    near_blocks = scatter_about(own_keys[5], (NCL, N_BLOCKS, NEAR_HALF, LEAF, LEAF), (LEAF * NEAR_HALF * N_BLOCKS) ** -0.5, 0.125, ((0, 8), (1, 2)))
    near_cols = draw_near_cols(jax.random.fold_in(jax.random.fold_in(keys[7], part), 71), part)
    return dict(adjoint_in=adjoint_in, far_u=far_u, far_v=far_v, far_cols=far_cols, far_counts=far_counts, near_blocks=near_blocks, near_cols=near_cols)


def reference(adjoint_in, far_u, far_v, far_cols, far_counts, near_blocks, near_cols):
    slot_ids = jnp.arange(FAR_HALF, dtype=jnp.int32)

    def row_step(totals, pieces):
        vector_row, u_blocks, v_blocks, targets, live_count, near_row, near_targets = pieces
        coefficients = jnp.einsum("bfkl,il->bfik", u_blocks.astype(jnp.float32), vector_row.astype(jnp.float32))
        coefficients = coefficients.astype(jnp.bfloat16)
        far_terms = jnp.einsum("bfik,bfkl->bfil", coefficients.astype(jnp.float32), v_blocks.astype(jnp.float32))
        live_slots = slot_ids[None, :] < live_count[:, None]
        far_terms = jnp.where(live_slots[:, :, None, None], far_terms, jnp.zeros_like(far_terms))
        totals = totals.at[targets.reshape(-1)].add(far_terms.reshape(-1, R, LEAF))
        near_terms = jnp.einsum("im,bjml->bjil", vector_row.astype(jnp.float32), near_row.astype(jnp.float32))
        totals = totals.at[near_targets.reshape(-1)].add(near_terms.reshape(-1, R, LEAF))
        return totals, None

    start = jnp.zeros((NCL, R, LEAF), dtype=jnp.float32)
    totals, _ = lax.scan(row_step, start, (adjoint_in, far_u, far_v, far_cols, far_counts, near_blocks, near_cols))
    return totals
```

```python
import functools
import math

import jax
import jax.numpy as jnp
from jax import lax
from jax.experimental import pallas as pl
from jax.experimental.pallas import tpu as pltpu
from jax.sharding import PartitionSpec as P

LANES = 128
CHUNKS = 4
UNROLLED = 16


def each(count, step):
    if count <= UNROLLED:
        for index in range(count):
            step(index)
    else:
        pl.loop(0, count)(step)


def product_kernel(
    row_count, block_count,
    vector_hbm, u_hbm, v_hbm, cols_hbm, counts_hbm, near_hbm, near_cols_hbm,
    out_ref,
    vector, u, v, near, cols, counts, near_cols, coefficients, partial,
    outgoing, incoming, load_sems, chunk_sems, send_sem, recv_sem,
):
    far_total, rank, width = u.shape
    near_total = near.shape[0]
    rhs_count = vector.shape[0]
    half = rhs_count // block_count
    pieces = width // LANES
    device_total = row_count * block_count
    me = lax.axis_index("rows") * block_count + lax.axis_index("blocks")
    chunk = far_total // CHUNKS
    depth = chunk * rank
    group = math.gcd(row_count, 8)

    def loaded(hbm, here, sem):
        copy = pltpu.make_async_copy(hbm, here, load_sems.at[sem])
        copy.start()
        return copy

    def chunk_loaded(hbm, here, part, which):
        slots = pl.ds(part * chunk, chunk)
        copy = pltpu.make_async_copy(
            hbm.at[0, 0, slots], here.at[slots], chunk_sems.at[which, part]
        )
        copy.start()
        return copy

    vector_copy = loaded(vector_hbm.at[0], vector, 0)
    cols_copy = loaded(cols_hbm, cols, 1)
    counts_copy = loaded(counts_hbm, counts, 2)
    near_cols_copy = loaded(near_cols_hbm, near_cols, 3)
    u_copies = [chunk_loaded(u_hbm, u, part, 0) for part in range(CHUNKS)]
    near_copy = loaded(near_hbm.at[0, 0], near, 4)
    v_copies = [chunk_loaded(v_hbm, v, part, 1) for part in range(CHUNKS)]

    def partner(distance):
        other = lax.rem(me + distance, device_total)
        return {"rows": other // block_count, "blocks": lax.rem(other, block_count)}

    barrier = pltpu.get_barrier_semaphore()

    def greet(index):
        pl.semaphore_signal(
            barrier, inc=1, device_id=partner(index + 1), device_id_type=pl.DeviceIdType.MESH
        )

    each(device_total - 1, greet)

    cols_copy.wait()
    counts_copy.wait()
    near_cols_copy.wait()
    live_count = counts[0, 0]
    vector_copy.wait()
    vector_row = vector[...]

    def slot_cols(part):
        lanes = lax.broadcasted_iota(jnp.int32, (rhs_count, LANES), 1)
        across = LANES // rank
        tiles = []
        for tile in range(depth // LANES):
            first = part * chunk + tile * across
            tile_cols = jnp.full((rhs_count, LANES), cols[0, 0, first], jnp.int32)
            for place in range(1, across):
                tile_cols = jnp.where(lanes >= place * rank, cols[0, 0, first + place], tile_cols)
            tiles.append(jnp.where(first + lanes // rank < live_count, tile_cols, -1))
        return jnp.concatenate(tiles, axis=1)

    def far_rows(part, first_cluster, chunk_coefficients):
        chunk_cols = slot_cols(part)
        rows = [
            jnp.where(chunk_cols == first_cluster + index, chunk_coefficients, 0.0)
            for index in range(group)
        ]
        return jnp.concatenate(rows, axis=0).astype(jnp.bfloat16)

    def chunk_coefficients(part):
        blocks = u[part * chunk:(part + 1) * chunk].reshape(depth, width)
        return lax.dot_general(
            vector_row, blocks, (((1,), (1,)), ((), ())), preferred_element_type=jnp.float32
        )

    def v_blocks(part):
        return v[part * chunk:(part + 1) * chunk].reshape(depth, width)

    def near_term(index):
        return jnp.dot(vector_row, near[index], preferred_element_type=jnp.float32)

    def near_sum(first_cluster, terms):
        rows = []
        for index in range(group):
            row = jnp.zeros((rhs_count, width), jnp.float32)
            for place in range(near_total):
                named = (near_cols[0, 0, place] == first_cluster + index).astype(jnp.float32)
                row = row + named * terms[place]
            rows.append(row)
        return jnp.concatenate(rows, axis=0)

    def put(first_cluster, total):
        first_row = first_cluster * rhs_count
        if not isinstance(first_row, int):
            first_row = pl.multiple_of(first_row, group * rhs_count)
        partial[pl.ds(first_row, group * rhs_count)] = total
        for index in range(group * block_count):
            rows = total[index * half:(index + 1) * half]
            outgoing[first_cluster * block_count + index] = jnp.concatenate(
                [rows[:, piece * LANES:(piece + 1) * LANES] for piece in range(pieces)], axis=0
            ).astype(jnp.bfloat16)

    if row_count == group:
        far = []
        for part in range(CHUNKS):
            u_copies[part].wait()
            far.append(far_rows(part, 0, chunk_coefficients(part)))
        near_copy.wait()
        total = near_sum(0, [near_term(index) for index in range(near_total)])
        for part in range(CHUNKS):
            v_copies[part].wait()
            total = total + jnp.dot(far[part], v_blocks(part), preferred_element_type=jnp.float32)
        put(0, total)
    else:
        for part in range(CHUNKS):
            u_copies[part].wait()
            coefficients[:, part * depth:(part + 1) * depth] = chunk_coefficients(part)
        near_copy.wait()
        for part in range(CHUNKS):
            v_copies[part].wait()

        @pl.loop(0, row_count // group)
        def _(step):
            first_cluster = step * group
            total = near_sum(first_cluster, [near_term(index) for index in range(near_total)])
            for part in range(CHUNKS):
                held = coefficients[:, part * depth:(part + 1) * depth]
                total = total + jnp.dot(
                    far_rows(part, first_cluster, held), v_blocks(part),
                    preferred_element_type=jnp.float32,
                )
            put(first_cluster, total)

    pl.semaphore_wait(barrier, device_total - 1)

    def send(index):
        distance = index + 1
        pltpu.make_async_remote_copy(
            src_ref=outgoing.at[lax.rem(me + distance, device_total)],
            dst_ref=incoming.at[index],
            send_sem=send_sem,
            recv_sem=recv_sem,
            device_id=partner(distance),
            device_id_type=pl.DeviceIdType.MESH,
        ).start()

    each(device_total - 1, send)

    own = partial[pl.ds(pl.multiple_of(me * half, half), half)]
    pltpu.make_async_copy(incoming, incoming, recv_sem).wait()
    arrived = jnp.sum(incoming[...].astype(jnp.float32), axis=0)
    out_ref[0] = own + jnp.concatenate(
        [arrived[piece * half:(piece + 1) * half] for piece in range(pieces)], axis=1
    )
    pltpu.make_async_copy(incoming, incoming, send_sem).wait()


def on_device(row_count, block_count, adjoint_in, far_u, far_v, far_cols, far_counts, near_blocks, near_cols):
    far_total, rank, width = far_u.shape[2:]
    rhs_count = adjoint_in.shape[1]
    half = rhs_count // block_count
    device_total = row_count * block_count
    message = (half * width // LANES, LANES)
    in_place = pl.BlockSpec(memory_space=pl.ANY)
    return pl.pallas_call(
        functools.partial(product_kernel, row_count, block_count),
        out_shape=jax.ShapeDtypeStruct((1, half, width), jnp.float32),
        in_specs=[in_place] * 7,
        out_specs=pl.BlockSpec(memory_space=pltpu.VMEM),
        scratch_shapes=[
            pltpu.VMEM((rhs_count, width), jnp.bfloat16),
            pltpu.VMEM((far_total, rank, width), jnp.bfloat16),
            pltpu.VMEM((far_total, rank, width), jnp.bfloat16),
            pltpu.VMEM(near_blocks.shape[2:], jnp.bfloat16),
            pltpu.SMEM(far_cols.shape, jnp.int32),
            pltpu.SMEM(far_counts.shape, jnp.int32),
            pltpu.SMEM(near_cols.shape, jnp.int32),
            pltpu.VMEM((rhs_count, far_total * rank), jnp.float32),
            pltpu.VMEM((row_count * rhs_count, width), jnp.float32),
            pltpu.VMEM((device_total,) + message, jnp.bfloat16),
            pltpu.VMEM((device_total - 1,) + message, jnp.bfloat16),
            pltpu.SemaphoreType.DMA((5,)),
            pltpu.SemaphoreType.DMA((2, CHUNKS)),
            pltpu.SemaphoreType.DMA,
            pltpu.SemaphoreType.DMA,
        ],
        compiler_params=pltpu.CompilerParams(
            collective_id=0, has_side_effects=True, vmem_limit_bytes=63 * 1024 * 1024
        ),
    )(adjoint_in, far_u, far_v, far_cols, far_counts, near_blocks, near_cols)


def solution(mesh):
    in_specs = (
        P(("groups", "rows"), None, None),
        P(("groups", "rows"), "blocks", None, None, None),
        P(("groups", "rows"), "blocks", None, None, None),
        P(("groups", "rows"), "blocks", None),
        P(("groups", "rows"), "blocks"),
        P(("groups", "rows"), "blocks", None, None, None),
        P(("groups", "rows"), "blocks", None),
    )
    out_specs = P(("groups", "rows"), "blocks", None)
    return jax.shard_map(
        functools.partial(on_device, mesh.shape["rows"], mesh.shape["blocks"]),
        mesh=mesh, in_specs=in_specs, out_specs=out_specs, check_vma=False,
    )
```

```python
import functools
import math

import jax
import jax.numpy as jnp
from jax import lax
from jax.experimental import pallas as pl
from jax.experimental.pallas import tpu as pltpu
from jax.sharding import PartitionSpec as P

LANES = 128
CHUNKS = 1
UNROLLED = 16


def each(count, step):
    if count <= UNROLLED:
        for index in range(count):
            step(index)
    else:
        pl.loop(0, count)(step)


def product_kernel(
    row_count, block_count,
    vector_hbm, u_hbm, v_hbm, cols_hbm, counts_hbm, near_hbm, near_cols_hbm,
    out_ref,
    vector, u, v, near, cols, counts, near_cols, masks, partial, load_sems, chunk_sems, send_sem, recv_sem,
):
    far_total, rank, width = u.shape
    near_total = near.shape[0]
    rhs_count = vector.shape[0]
    half = rhs_count // block_count
    device_total = row_count * block_count
    me = lax.axis_index("rows") * block_count + lax.axis_index("blocks")
    chunk = far_total // CHUNKS
    depth = chunk * rank
    group = math.gcd(row_count, 8)

    def loaded(hbm, here, sem):
        copy = pltpu.make_async_copy(hbm, here, load_sems.at[sem])
        copy.start()
        return copy

    def chunk_loaded(hbm, here, part, which):
        slots = pl.ds(part * chunk, chunk)
        copy = pltpu.make_async_copy(
            hbm.at[0, 0, slots], here.at[slots], chunk_sems.at[which, part]
        )
        copy.start()
        return copy

    vector_copy = loaded(vector_hbm.at[0], vector, 0)
    cols_copy = loaded(cols_hbm, cols, 1)
    counts_copy = loaded(counts_hbm, counts, 2)
    near_cols_copy = loaded(near_cols_hbm, near_cols, 3)
    u_copies = [chunk_loaded(u_hbm, u, part, 0) for part in range(CHUNKS)]
    near_copy = loaded(near_hbm.at[0, 0], near, 4)
    v_copies = [chunk_loaded(v_hbm, v, part, 1) for part in range(CHUNKS)]

    row = lax.axis_index("rows")
    block = lax.axis_index("blocks")

    def partner(distance):
        return {
            "rows": lax.rem(row + distance // block_count, row_count),
            "blocks": lax.rem(block + distance % block_count, block_count),
        }

    barrier = pltpu.get_barrier_semaphore()

    def greet(index):
        pl.semaphore_signal(
            barrier, inc=1, device_id=partner(index + 1), device_id_type=pl.DeviceIdType.MESH
        )

    each(device_total - 1, greet)

    cols_copy.wait()
    counts_copy.wait()
    near_cols_copy.wait()
    live_count = counts[0, 0]
    vector_copy.wait()
    vector_row = vector[...]

    def slot_cols(part):
        lanes = lax.broadcasted_iota(jnp.int32, (rhs_count, LANES), 1)
        across = LANES // rank
        tiles = []
        for tile in range(depth // LANES):
            first = part * chunk + tile * across
            tile_cols = jnp.full((rhs_count, LANES), cols[0, 0, first], jnp.int32)
            for place in range(1, across):
                tile_cols = jnp.where(lanes >= place * rank, cols[0, 0, first + place], tile_cols)
            tiles.append(jnp.where(first + lanes // rank < live_count, tile_cols, -1))
        return jnp.concatenate(tiles, axis=1)

    def put_masks(first_cluster):
        for part in range(CHUNKS):
            part_cols = slot_cols(part)
            for index in range(group):
                masks[index, :, part * depth:(part + 1) * depth] = jnp.where(
                    part_cols == first_cluster + index, 1.0, 0.0
                ).astype(jnp.bfloat16)

    def far_rows(part, coefficients):
        return jnp.concatenate(
            [coefficients * masks[index, :, part * depth:(part + 1) * depth] for index in range(group)],
            axis=0,
        )

    def chunk_coefficients(part):
        blocks = u[part * chunk:(part + 1) * chunk].reshape(depth, width)
        return lax.dot_general(
            vector_row, blocks, (((1,), (1,)), ((), ())), preferred_element_type=jnp.float32
        ).astype(jnp.bfloat16)

    def v_blocks(part):
        return v[part * chunk:(part + 1) * chunk].reshape(depth, width)

    def near_term(index):
        return jnp.dot(vector_row, near[index], preferred_element_type=jnp.float32)

    def near_sum(first_cluster, terms):
        rows = []
        for index in range(group):
            row = jnp.zeros((rhs_count, width), jnp.float32)
            for place in range(near_total):
                named = (near_cols[0, 0, place] == first_cluster + index).astype(jnp.float32)
                row = row + named * terms[place]
            rows.append(row)
        return jnp.concatenate(rows, axis=0)

    def put(first_cluster, total):
        first_row = first_cluster * rhs_count
        if not isinstance(first_row, int):
            first_row = pl.multiple_of(first_row, group * rhs_count)
        partial[pl.ds(first_row, group * rhs_count)] = total

    if row_count == group:
        put_masks(0)
        far = []
        for part in range(CHUNKS):
            u_copies[part].wait()
            far.append(far_rows(part, chunk_coefficients(part)))
        near_copy.wait()
        total = near_sum(0, [near_term(index) for index in range(near_total)])
        for part in range(CHUNKS):
            v_copies[part].wait()
            total = total + jnp.concatenate([
                jnp.dot(far[part], v_blocks(part)[:, piece:piece + LANES], preferred_element_type=jnp.float32)
                for piece in range(0, width, LANES)
            ], axis=1)
        put(0, total)
    else:
        near_copy.wait()
        for part in range(CHUNKS):
            u_copies[part].wait()
            v_copies[part].wait()

        @pl.loop(0, row_count // group)
        def _(step):
            first_cluster = step * group
            put_masks(first_cluster)
            total = near_sum(first_cluster, [near_term(index) for index in range(near_total)])
            for part in range(CHUNKS):
                total = total + jnp.dot(
                    far_rows(part, chunk_coefficients(part)), v_blocks(part),
                    preferred_element_type=jnp.float32,
                )
            put(first_cluster, total)

    pl.semaphore_wait(barrier, device_total - 1)

    def rows_of(device):
        return partial.at[pl.ds(pl.multiple_of(device * half, half), half)]

    def send(index):
        other = partner(index + 1)
        pltpu.make_async_remote_copy(
            src_ref=rows_of(other["rows"] * block_count + other["blocks"]),
            dst_ref=out_ref.at[index],
            send_sem=send_sem,
            recv_sem=recv_sem,
            device_id=other,
            device_id_type=pl.DeviceIdType.MESH,
        ).start()

    each(device_total - 1, send)

    own_copy = loaded(rows_of(me), out_ref.at[device_total - 1], 0)
    arrivals = out_ref.at[pl.ds(0, device_total - 1)]
    pltpu.make_async_copy(arrivals, arrivals, recv_sem).wait()
    pltpu.make_async_copy(arrivals, arrivals, send_sem).wait()
    own_copy.wait()


def on_device(row_count, block_count, adjoint_in, far_u, far_v, far_cols, far_counts, near_blocks, near_cols):
    far_total, rank, width = far_u.shape[2:]
    rhs_count = adjoint_in.shape[1]
    half = rhs_count // block_count
    device_total = row_count * block_count
    in_place = pl.BlockSpec(memory_space=pl.ANY)
    received = pl.pallas_call(
        functools.partial(product_kernel, row_count, block_count),
        out_shape=jax.ShapeDtypeStruct((device_total, half, width), jnp.float32),
        in_specs=[in_place] * 7,
        out_specs=in_place,
        scratch_shapes=[
            pltpu.VMEM((rhs_count, width), jnp.bfloat16),
            pltpu.VMEM((far_total, rank, width), jnp.bfloat16),
            pltpu.VMEM((far_total, rank, width), jnp.bfloat16),
            pltpu.VMEM(near_blocks.shape[2:], jnp.bfloat16),
            pltpu.SMEM(far_cols.shape, jnp.int32),
            pltpu.SMEM(far_counts.shape, jnp.int32),
            pltpu.SMEM(near_cols.shape, jnp.int32),
            pltpu.VMEM((math.gcd(row_count, 8), rhs_count, far_total * rank), jnp.bfloat16),
            pltpu.VMEM((row_count * rhs_count, width), jnp.float32),
            pltpu.SemaphoreType.DMA((5,)),
            pltpu.SemaphoreType.DMA((2, CHUNKS)),
            pltpu.SemaphoreType.DMA,
            pltpu.SemaphoreType.DMA,
        ],
        compiler_params=pltpu.CompilerParams(
            collective_id=0, has_side_effects=True, vmem_limit_bytes=63 * 1024 * 1024
        ),
    )(adjoint_in, far_u, far_v, far_cols, far_counts, near_blocks, near_cols)
    return jnp.sum(received, axis=0, keepdims=True)


def solution(mesh):
    in_specs = (
        P(("groups", "rows"), None, None),
        P(("groups", "rows"), "blocks", None, None, None),
        P(("groups", "rows"), "blocks", None, None, None),
        P(("groups", "rows"), "blocks", None),
        P(("groups", "rows"), "blocks"),
        P(("groups", "rows"), "blocks", None, None, None),
        P(("groups", "rows"), "blocks", None),
    )
    out_specs = P(("groups", "rows"), "blocks", None)
    return jax.shard_map(
        functools.partial(on_device, mesh.shape["rows"], mesh.shape["blocks"]),
        mesh=mesh, in_specs=in_specs, out_specs=out_specs, check_vma=False,
    )
```

```python
import functools
import math

import jax
import jax.numpy as jnp
from jax import lax
from jax.experimental import pallas as pl
from jax.experimental.pallas import tpu as pltpu
from jax.sharding import PartitionSpec as P

LANES = 128
CHUNKS = 2
UNROLLED = 16


def each(count, step):
    if count <= UNROLLED:
        for index in range(count):
            step(index)
    else:
        pl.loop(0, count)(step)


def product_kernel(
    row_count, block_count,
    vector_hbm, u_hbm, v_hbm, cols_hbm, counts_hbm, near_hbm, near_cols_hbm,
    out_ref,
    vector, u, v, near, cols, counts, near_cols, masks, far, partial, load_sems, chunk_sems, send_sem, recv_sem,
):
    far_total, rank, width = u.shape
    near_total = near.shape[0]
    rhs_count = vector.shape[0]
    half = rhs_count // block_count
    device_total = row_count * block_count
    me = lax.axis_index("rows") * block_count + lax.axis_index("blocks")
    chunk = far_total // CHUNKS
    depth = chunk * rank
    group = math.gcd(row_count, 8)

    def loaded(hbm, here, sem):
        copy = pltpu.make_async_copy(hbm, here, load_sems.at[sem])
        copy.start()
        return copy

    def chunk_loaded(hbm, here, part, which):
        slots = pl.ds(part * chunk, chunk)
        copy = pltpu.make_async_copy(
            hbm.at[0, 0, slots], here.at[slots], chunk_sems.at[which, part]
        )
        copy.start()
        return copy

    vector_copy = loaded(vector_hbm.at[0], vector, 0)
    cols_copy = loaded(cols_hbm, cols, 1)
    counts_copy = loaded(counts_hbm, counts, 2)
    near_cols_copy = loaded(near_cols_hbm, near_cols, 3)
    u_copies = [chunk_loaded(u_hbm, u, part, 0) for part in range(CHUNKS)]
    near_copy = loaded(near_hbm.at[0, 0], near, 4)
    v_copies = [chunk_loaded(v_hbm, v, part, 1) for part in range(CHUNKS)]

    row = lax.axis_index("rows")
    block = lax.axis_index("blocks")

    def partner(distance):
        return {
            "rows": lax.rem(row + distance // block_count, row_count),
            "blocks": lax.rem(block + distance % block_count, block_count),
        }

    barrier = pltpu.get_barrier_semaphore()

    def greet(index):
        pl.semaphore_signal(
            barrier, inc=1, device_id=partner(index + 1), device_id_type=pl.DeviceIdType.MESH
        )

    each(device_total - 1, greet)

    cols_copy.wait()
    counts_copy.wait()
    near_cols_copy.wait()
    live_count = counts[0, 0]
    vector_copy.wait()
    vector_row = vector[...]

    def slot_cols(part):
        lanes = lax.broadcasted_iota(jnp.int32, (rhs_count, LANES), 1)
        across = LANES // rank
        tiles = []
        for tile in range(depth // LANES):
            first = part * chunk + tile * across
            tile_cols = jnp.full((rhs_count, LANES), cols[0, 0, first], jnp.int32)
            for place in range(1, across):
                tile_cols = jnp.where(lanes >= place * rank, cols[0, 0, first + place], tile_cols)
            tiles.append(jnp.where(first + lanes // rank < live_count, tile_cols, -1))
        return jnp.concatenate(tiles, axis=1)

    def put_masks(first_cluster):
        for part in range(CHUNKS):
            part_cols = slot_cols(part)
            for index in range(group):
                masks[index, :, part * depth:(part + 1) * depth] = jnp.where(
                    part_cols == first_cluster + index, 1.0, 0.0
                ).astype(jnp.bfloat16)

    def far_rows(part, coefficients):
        return jnp.concatenate(
            [coefficients * masks[index, :, part * depth:(part + 1) * depth] for index in range(group)],
            axis=0,
        )

    def chunk_coefficients(part):
        blocks = u[part * chunk:(part + 1) * chunk].reshape(depth, width)
        return lax.dot_general(
            vector_row, blocks, (((1,), (1,)), ((), ())), preferred_element_type=jnp.float32
        ).astype(jnp.bfloat16)

    def v_blocks(part):
        return v[part * chunk:(part + 1) * chunk].reshape(depth, width)

    def near_term(index):
        return jnp.dot(vector_row, near[index], preferred_element_type=jnp.float32)

    def near_sum(first_cluster, terms):
        rows = []
        for index in range(group):
            row = jnp.zeros((rhs_count, width), jnp.float32)
            for place in range(near_total):
                named = (near_cols[0, 0, place] == first_cluster + index).astype(jnp.float32)
                row = row + named * terms[place]
            rows.append(row)
        return jnp.concatenate(rows, axis=0)

    def put(first_cluster, total):
        first_row = first_cluster * rhs_count
        if not isinstance(first_row, int):
            first_row = pl.multiple_of(first_row, group * rhs_count)
        partial[pl.ds(first_row, group * rhs_count)] = total

    if row_count == group:
        put_masks(0)
        for part in range(CHUNKS):
            u_copies[part].wait()
            far[:, part * depth:(part + 1) * depth] = far_rows(part, chunk_coefficients(part))
        near_copy.wait()
        total = near_sum(0, [near_term(index) for index in range(near_total)])
        for part in range(CHUNKS):
            v_copies[part].wait()
            total = total + jnp.concatenate([
                jnp.dot(
                    far[:, part * depth:(part + 1) * depth], v_blocks(part)[:, piece:piece + LANES],
                    preferred_element_type=jnp.float32,
                )
                for piece in range(0, width, LANES)
            ], axis=1)
        put(0, total)
    else:
        near_copy.wait()
        for part in range(CHUNKS):
            u_copies[part].wait()
            v_copies[part].wait()

        @pl.loop(0, row_count // group)
        def _(step):
            first_cluster = step * group
            put_masks(first_cluster)
            total = near_sum(first_cluster, [near_term(index) for index in range(near_total)])
            for part in range(CHUNKS):
                total = total + jnp.dot(
                    far_rows(part, chunk_coefficients(part)), v_blocks(part),
                    preferred_element_type=jnp.float32,
                )
            put(first_cluster, total)

    pl.semaphore_wait(barrier, device_total - 1)

    def rows_of(device):
        return partial.at[pl.ds(pl.multiple_of(device * half, half), half)]

    def send(index):
        other = partner(index + 1)
        pltpu.make_async_remote_copy(
            src_ref=rows_of(other["rows"] * block_count + other["blocks"]),
            dst_ref=out_ref.at[index],
            send_sem=send_sem,
            recv_sem=recv_sem,
            device_id=other,
            device_id_type=pl.DeviceIdType.MESH,
        ).start()

    each(device_total - 1, send)

    own_copy = loaded(rows_of(me), out_ref.at[device_total - 1], 0)
    arrivals = out_ref.at[pl.ds(0, device_total - 1)]
    pltpu.make_async_copy(arrivals, arrivals, recv_sem).wait()
    pltpu.make_async_copy(arrivals, arrivals, send_sem).wait()
    own_copy.wait()


def on_device(row_count, block_count, adjoint_in, far_u, far_v, far_cols, far_counts, near_blocks, near_cols):
    far_total, rank, width = far_u.shape[2:]
    rhs_count = adjoint_in.shape[1]
    half = rhs_count // block_count
    device_total = row_count * block_count
    in_place = pl.BlockSpec(memory_space=pl.ANY)
    received = pl.pallas_call(
        functools.partial(product_kernel, row_count, block_count),
        out_shape=jax.ShapeDtypeStruct((device_total, half, width), jnp.float32),
        in_specs=[in_place] * 7,
        out_specs=in_place,
        scratch_shapes=[
            pltpu.VMEM((rhs_count, width), jnp.bfloat16),
            pltpu.VMEM((far_total, rank, width), jnp.bfloat16),
            pltpu.VMEM((far_total, rank, width), jnp.bfloat16),
            pltpu.VMEM(near_blocks.shape[2:], jnp.bfloat16),
            pltpu.SMEM(far_cols.shape, jnp.int32),
            pltpu.SMEM(far_counts.shape, jnp.int32),
            pltpu.SMEM(near_cols.shape, jnp.int32),
            pltpu.VMEM((math.gcd(row_count, 8), rhs_count, far_total * rank), jnp.bfloat16),
            pltpu.VMEM((math.gcd(row_count, 8) * rhs_count, far_total * rank), jnp.bfloat16),
            pltpu.VMEM((row_count * rhs_count, width), jnp.float32),
            pltpu.SemaphoreType.DMA((5,)),
            pltpu.SemaphoreType.DMA((2, CHUNKS)),
            pltpu.SemaphoreType.DMA,
            pltpu.SemaphoreType.DMA,
        ],
        compiler_params=pltpu.CompilerParams(
            collective_id=0, has_side_effects=True, vmem_limit_bytes=63 * 1024 * 1024
        ),
    )(adjoint_in, far_u, far_v, far_cols, far_counts, near_blocks, near_cols)
    return jnp.sum(received, axis=0, keepdims=True)


def solution(mesh):
    in_specs = (
        P(("groups", "rows"), None, None),
        P(("groups", "rows"), "blocks", None, None, None),
        P(("groups", "rows"), "blocks", None, None, None),
        P(("groups", "rows"), "blocks", None),
        P(("groups", "rows"), "blocks"),
        P(("groups", "rows"), "blocks", None, None, None),
        P(("groups", "rows"), "blocks", None),
    )
    out_specs = P(("groups", "rows"), "blocks", None)
    return jax.shard_map(
        functools.partial(on_device, mesh.shape["rows"], mesh.shape["blocks"]),
        mesh=mesh, in_specs=in_specs, out_specs=out_specs, check_vma=False,
    )
```
